32 devices in a mesh: groups: 2 (over x), gx: 4 (over y, core), gy: 4 (over z).
Axes of the slice: x: 2, y: 2, z: 4, core: 2. Of those that a mesh axis runs over, the one named last changes fastest.
Arguments:
- tokens: bfloat16 [1024, 6144], P(('groups', 'gy'), 'gx'), parts along dimension 0, may hold values from -6 to 6
- w_in: bfloat16 [6144, 24576], P('gx', 'gy'), may hold values from -0.078125 to 0.078125
- w_out: bfloat16 [24576, 6144], P('gy', 'gx'), may hold values from -0.0390625 to 0.0390625
- grad_out: bfloat16 [1024, 6144], P(('groups', 'gy'), 'gx'), parts along dimension 0, may hold values from -1.1953125 to 1.1953125
Outputs:
- output: bfloat16 [1024, 6144], P(('groups', 'gy'), 'gx'), parts along dimension 0
- grad_tokens: bfloat16 [1024, 6144], P(('groups', 'gy'), 'gx'), parts along dimension 0
- grad_w_in: bfloat16 [12288, 24576], P(('groups', 'gx'), 'gy'), parts along dimension 0
- grad_w_out: bfloat16 [49152, 6144], P(('groups', 'gy'), 'gx'), parts along dimension 0
The draws below stay inside these ranges and needn't reach their ends.
There are 2 independent parts, one for each index of `groups`. The reference program is written for one: setup_inputs(seed, part) draws one part's arguments, and reference() takes and returns one part's arrays. A program takes and returns all parts, laid end to end along the dimension named above; an argument that names none is the same for every part. Nothing has to cross between parts.
All inputs are finite; a program needn't handle non-finite values.
Results may differ from the reference program's by a relative error of at most 0.018.
Values may be sent and summed in bfloat16 or wider, within the bound.
A program may use at most 192 MiB of HBM per device.

```python
import jax
import jax.numpy as jnp
from jax import lax

D = 6144
FF = 24576
TOKENS = 512
N_GX = 4
N_GY = 4


def shard_levels(stream_key, shape, split, low, top_value):
    def one(position, blocks):
        draws = jax.random.uniform(jax.random.fold_in(jax.random.fold_in(stream_key, 6), position), (blocks,), jnp.float32, low / len(split), top_value / len(split))
        return jnp.repeat(jnp.exp(draws), shape[position] // blocks).reshape((-1,) + (1,) * (len(shape) - position - 1))

    level = one(*split[0])
    for cut in split[1:]:
        level = level * one(*cut)
    return level


def normal_values(own_key, shape, spread, most, cuts=(), dtype=jnp.bfloat16):
    values = jax.random.normal(own_key, shape, jnp.float32) * spread
    if len(cuts) > 0:
        values = shard_levels(own_key, shape, cuts, -0.22, 0.18) * values
    return jnp.clip(values, min=-most, max=most).astype(dtype)


def setup_inputs(seed: int = 0, part: int = 0) -> dict:
    key_list = jax.random.split(jax.random.key(seed), 5)
    part_splits = jax.random.split(jax.random.fold_in(key_list[4], part), 5)
    return {
        "tokens": normal_values(part_splits[0], (TOKENS, D), 1.0, 6.0, ((0, 4), (1, 4))),
        "w_in": normal_values(key_list[1], (D, FF), D ** -0.5, 0.078125, ((0, 4), (1, 4))),
        "w_out": normal_values(key_list[2], (FF, D), FF ** -0.5, 0.0390625, ((0, 4), (1, 4))),
        "grad_out": normal_values(part_splits[3], (TOKENS, D), 0.2, 1.1953125, ((0, 4), (1, 4))),
    }


def gelu_slope(value):
    coeff = 0.7978845608028654
    inner = coeff * (value + 0.044715 * value * value * value)
    tanh_val = jnp.tanh(inner)
    return 0.5 * (1.0 + tanh_val) + 0.5 * value * (1.0 - tanh_val * tanh_val) * coeff * (1.0 + 3.0 * 0.044715 * value * value)


def block_sum(left_mat, right_mat, blocks):
    rows = left_mat.shape[0]
    inner = left_mat.shape[1]
    width = right_mat.shape[1]
    left_parts = left_mat.reshape(rows, blocks, inner // blocks).transpose(1, 0, 2)
    right_parts = right_mat.reshape(blocks, inner // blocks, width)

    def add_block(total, pair):
        product = jnp.dot(pair[0], pair[1], preferred_element_type=jnp.float32).astype(jnp.bfloat16)
        product = lax.optimization_barrier(product)
        return total + product.astype(jnp.float32), None

    start = jnp.zeros((rows, width), jnp.float32)
    total, unused = lax.scan(add_block, start, (left_parts, right_parts))
    return total


def reference(tokens, w_in, w_out, grad_out):
    pre_act = block_sum(tokens, w_in, N_GX)
    hidden = jax.nn.gelu(pre_act, approximate=True).astype(jnp.bfloat16)
    output = block_sum(hidden, w_out, N_GY).astype(jnp.bfloat16)
    grad_hidden = block_sum(grad_out, w_out.T, N_GX)
    grad_pre = (grad_hidden * gelu_slope(pre_act)).astype(jnp.bfloat16)
    grad_w_out = jnp.dot(hidden.T, grad_out, preferred_element_type=jnp.float32).astype(jnp.bfloat16)
    grad_w_in = jnp.dot(tokens.T, grad_pre, preferred_element_type=jnp.float32).astype(jnp.bfloat16)
    grad_tokens = block_sum(grad_pre, w_in.T, N_GY).astype(jnp.bfloat16)
    return (output, grad_tokens, grad_w_in, grad_w_out)
```

```python
import jax
import jax.numpy as jnp
from jax import lax
from jax.sharding import PartitionSpec as P


def gelu_slope(value):
    coeff = 0.7978845608028654
    inner = coeff * (value + 0.044715 * value * value * value)
    tanh_val = jnp.tanh(inner)
    return 0.5 * (1.0 + tanh_val) + 0.5 * value * (1.0 - tanh_val * tanh_val) * coeff * (
        1.0 + 3.0 * 0.044715 * value * value
    )


def product(left_mat, right_mat, flipped):
    if flipped:
        return lax.dot_general(
            left_mat, right_mat, (((1,), (1,)), ((), ())), preferred_element_type=jnp.float32
        )
    return jnp.dot(left_mat, right_mat, preferred_element_type=jnp.float32)


def inner_rows(left_mat, right_mat):
    return lax.dot_general(
        left_mat, right_mat, (((0,), (0,)), ((), ())), preferred_element_type=jnp.float32
    )


def general_shards(tokens, w_in, w_out, grad_out):
    def token_gather(local_rows):
        return lax.all_gather(local_rows, "gy", axis=0, tiled=True)

    def token_total(term):
        return lax.psum_scatter(term.astype(jnp.bfloat16), "gy", scatter_dimension=0, tiled=True)

    def hidden_sum(left_mat, right_mat, flipped):
        return lax.psum_scatter(
            product(left_mat, right_mat, flipped).astype(jnp.bfloat16),
            "gx",
            scatter_dimension=1,
            tiled=True,
        ).astype(jnp.float32)

    def hidden_gather(share_part):
        return lax.all_gather(share_part, "gx", axis=1, tiled=True)

    rows_in = token_gather(tokens)
    pre_act = hidden_sum(rows_in, w_in, False)
    hidden = jax.nn.gelu(pre_act, approximate=True).astype(jnp.bfloat16)
    hidden_all = hidden_gather(hidden)
    output = token_total(product(hidden_all, w_out, False))
    grads_in = token_gather(grad_out)
    grad_hidden = hidden_sum(grads_in, w_out, True)
    grad_pre = (grad_hidden * gelu_slope(pre_act)).astype(jnp.bfloat16)
    grad_all = hidden_gather(grad_pre)
    grad_w_out = inner_rows(hidden_all, grads_in).astype(jnp.bfloat16)
    grad_w_in = inner_rows(rows_in, grad_all).astype(jnp.bfloat16)
    grad_tokens = token_total(product(grad_all, w_in, True))
    return (output, grad_tokens, grad_w_in, grad_w_out)


CHUNKS = 4


def square_shards(n_gy, tokens, w_in, w_out, grad_out):
    bf16, f32 = jnp.bfloat16, jnp.float32
    ff = w_in.shape[1]
    width = ff // CHUNKS
    half = width // 2
    core = lax.axis_index("gx") % 2
    is_first = core == 0
    forward = [(i, (i + 1) % n_gy) for i in range(n_gy)]
    backward = [(i, (i + n_gy - 1) % n_gy) for i in range(n_gy)]
    sibling = [(i, i ^ 1) for i in range(4)]
    across = [(i, i ^ 2) for i in range(4)]

    def ring_gather(block):
        blocks = [block]
        for _ in range(n_gy - 1):
            blocks.append(lax.ppermute(blocks[-1], "gy", forward))
        return blocks

    def chip_sum(partial):
        first, second = partial[:, :half], partial[:, half:]
        kept = jnp.where(is_first, first, second)
        given = jnp.where(is_first, second, first).astype(bf16)
        total = kept + lax.ppermute(given, "gx", sibling).astype(f32)
        return total.astype(bf16)

    def full_sum(partial):
        mine = chip_sum(partial)
        return mine.astype(f32) + lax.ppermute(mine, "gx", across).astype(f32)

    def share(part):
        other = lax.ppermute(part, "gx", sibling)
        return jnp.concatenate(
            [jnp.where(is_first, part, other), jnp.where(is_first, other, part)], axis=1
        )

    token_blocks = ring_gather(tokens)
    grad_blocks = ring_gather(grad_out)
    n_half = n_gy // 2
    rows = tokens.shape[0]
    groups = [list(range(n_half)), list(range(n_half, n_gy))]
    token_rows = [jnp.concatenate([token_blocks[r] for r in g]) for g in groups]
    grad_rows = [jnp.concatenate([grad_blocks[r] for r in g]) for g in groups]

    pre = [[None] * CHUNKS for _ in groups]
    hidden = [[None] * CHUNKS for _ in groups]
    for g in (0, 1):
        for c in range(CHUNKS):
            part = product(token_rows[g], w_in[:, c * width : (c + 1) * width], False)
            pre[g][c] = full_sum(part)
            hidden[g][c] = share(jax.nn.gelu(pre[g][c], approximate=True).astype(bf16))
    grad_pre = [[None] * CHUNKS for _ in groups]
    for g in (1, 0):
        for c in range(CHUNKS):
            part = product(grad_rows[g], w_out[c * width : (c + 1) * width, :], True)
            slope = gelu_slope(pre[g][c])
            grad_pre[g][c] = share((full_sum(part) * slope).astype(bf16))

    def ring_total(terms):
        moving = terms[n_gy - 1]
        for r in range(n_gy - 2, -1, -1):
            moving = (
                lax.ppermute(moving.astype(bf16), "gy", backward).astype(f32) + terms[r]
            )
        return moving.astype(bf16)

    def cut(groups_terms):
        return [
            groups_terms[r // n_half][(r % n_half) * rows : (r % n_half + 1) * rows]
            .astype(bf16)
            .astype(f32)
            for r in range(n_gy)
        ]

    hidden_rows = [jnp.concatenate(h, axis=1) for h in hidden]
    output = ring_total(cut([product(h, w_out, False) for h in hidden_rows]))
    grads_all = [jnp.concatenate(h, axis=1) for h in grad_pre]
    grad_tokens = ring_total(cut([product(h, w_in, True) for h in grads_all]))
    grad_w_out = inner_rows(jnp.concatenate(hidden_rows), jnp.concatenate(grad_rows)).astype(bf16)
    grad_w_in = inner_rows(jnp.concatenate(token_rows), jnp.concatenate(grads_all)).astype(bf16)
    return (output, grad_tokens, grad_w_in, grad_w_out)


def solution(mesh):
    in_specs = (P(("groups", "gy"), "gx"), P("gx", "gy"), P("gy", "gx"), P(("groups", "gy"), "gx"))
    out_specs = (
        P(("groups", "gy"), "gx"),
        P(("groups", "gy"), "gx"),
        P(("groups", "gx"), "gy"),
        P(("groups", "gy"), "gx"),
    )
    n_gy = mesh.shape["gy"]
    if mesh.shape["gx"] == 4 and n_gy % 2 == 0:
        shards = lambda *arrays: square_shards(n_gy, *arrays)
    else:
        shards = general_shards
    return jax.shard_map(shards, mesh=mesh, in_specs=in_specs, out_specs=out_specs, check_vma=False)
```

```python
import jax
import jax.numpy as jnp
from jax import lax
from jax.sharding import PartitionSpec as P


def gelu_slope(value):
    coeff = 0.7978845608028654
    inner = coeff * (value + 0.044715 * value * value * value)
    tanh_val = jnp.tanh(inner)
    return 0.5 * (1.0 + tanh_val) + 0.5 * value * (1.0 - tanh_val * tanh_val) * coeff * (
        1.0 + 3.0 * 0.044715 * value * value
    )


def product(left_mat, right_mat, flipped):
    if flipped:
        return lax.dot_general(
            left_mat, right_mat, (((1,), (1,)), ((), ())), preferred_element_type=jnp.float32
        )
    return jnp.dot(left_mat, right_mat, preferred_element_type=jnp.float32)


def inner_rows(left_mat, right_mat):
    return lax.dot_general(
        left_mat, right_mat, (((0,), (0,)), ((), ())), preferred_element_type=jnp.float32
    )


def general_shards(tokens, w_in, w_out, grad_out):
    def token_gather(local_rows):
        return lax.all_gather(local_rows, "gy", axis=0, tiled=True)

    def token_total(term):
        return lax.psum_scatter(term.astype(jnp.bfloat16), "gy", scatter_dimension=0, tiled=True)

    def hidden_sum(left_mat, right_mat, flipped):
        return lax.psum_scatter(
            product(left_mat, right_mat, flipped).astype(jnp.bfloat16),
            "gx",
            scatter_dimension=1,
            tiled=True,
        ).astype(jnp.float32)

    def hidden_gather(share_part):
        return lax.all_gather(share_part, "gx", axis=1, tiled=True)

    rows_in = token_gather(tokens)
    pre_act = hidden_sum(rows_in, w_in, False)
    hidden = jax.nn.gelu(pre_act, approximate=True).astype(jnp.bfloat16)
    hidden_all = hidden_gather(hidden)
    output = token_total(product(hidden_all, w_out, False))
    grads_in = token_gather(grad_out)
    grad_hidden = hidden_sum(grads_in, w_out, True)
    grad_pre = (grad_hidden * gelu_slope(pre_act)).astype(jnp.bfloat16)
    grad_all = hidden_gather(grad_pre)
    grad_w_out = inner_rows(hidden_all, grads_in).astype(jnp.bfloat16)
    grad_w_in = inner_rows(rows_in, grad_all).astype(jnp.bfloat16)
    grad_tokens = token_total(product(grad_all, w_in, True))
    return (output, grad_tokens, grad_w_in, grad_w_out)


CHUNKS = 4
SPLIT_CHUNKS = 2
DEPTH = 3


def after(value, earlier):
    return lax.optimization_barrier((value, earlier))


def square_shards(n_gy, tokens, w_in, w_out, grad_out):
    bf16, f32 = jnp.bfloat16, jnp.float32
    width = w_in.shape[1] // CHUNKS
    half = width // 2
    rows = tokens.shape[0]
    is_first = lax.axis_index("gx") % 2 == 0
    forward = [(i, (i + 1) % n_gy) for i in range(n_gy)]
    backward = [(i, (i + n_gy - 1) % n_gy) for i in range(n_gy)]
    sibling = [(i, i ^ 1) for i in range(4)]
    across = [(i, i ^ 2) for i in range(4)]

    def ring_gather(block):
        blocks = [block]
        for _ in range(n_gy - 1):
            blocks.append(lax.ppermute(blocks[-1], "gy", forward))
        return blocks

    crossed = []

    def full_sum(left_mat, right_mat, flipped):
        if len(crossed) >= DEPTH:
            left_mat, crossed[-DEPTH][1] = after(left_mat, crossed[-DEPTH][1])
        partial = product(left_mat, right_mat, flipped).astype(bf16)
        first, second = partial[:, :half], partial[:, half:]
        kept = jnp.where(is_first, first, second).astype(f32)
        given = jnp.where(is_first, second, first)
        mine = (kept + lax.ppermute(given, "gx", sibling).astype(f32)).astype(bf16)
        crossed.append([mine, lax.ppermute(mine, "gx", across)])
        return crossed[-1]

    def added(pair):
        return pair[0].astype(f32) + pair[1].astype(f32)

    def share(part):
        other = lax.ppermute(part, "gx", sibling)
        return jnp.concatenate(
            [jnp.where(is_first, part, other), jnp.where(is_first, other, part)], axis=1
        )

    def ring_total(term, beside=None):
        parts = [term[r * rows : (r + 1) * rows].astype(bf16).astype(f32) for r in range(n_gy)]
        moving = parts[n_gy - 1]
        for r in range(n_gy - 2, -1, -1):
            if beside is not None and r == n_gy - 3:
                parts[r], beside = after(parts[r], beside)
            moving = lax.ppermute(moving.astype(bf16), "gy", backward).astype(f32) + parts[r]
        return moving.astype(bf16), beside

    token_blocks = ring_gather(tokens)
    grad_start, token_blocks[1] = after(grad_out, token_blocks[1])
    grad_blocks = ring_gather(grad_start)
    n_half = n_gy // 2
    near = jnp.concatenate(token_blocks[:n_half])
    far = jnp.concatenate(token_blocks[n_half:])
    token_rows = jnp.concatenate([near, far])
    grad_rows = jnp.concatenate(grad_blocks)

    def columns(c):
        return w_in[:, c * width : (c + 1) * width]

    def activated(pairs):
        pre = jnp.concatenate([added(p) for p in pairs])
        return pre, share(jax.nn.gelu(pre, approximate=True).astype(bf16))

    def grad_pair(c):
        return full_sum(grad_rows, w_out[c * width : (c + 1) * width, :], True)

    pairs = [[full_sum(near, columns(c), False)] for c in range(SPLIT_CHUNKS)]
    for c in range(SPLIT_CHUNKS):
        pairs[c].append(full_sum(far, columns(c), False))
    for c in range(SPLIT_CHUNKS, CHUNKS):
        pairs.append([full_sum(token_rows, columns(c), False)])
    grad_pairs = [grad_pair(0), grad_pair(1)]
    pre, hidden = zip(*[activated(p) for p in pairs])
    hidden_all = jnp.concatenate(hidden, axis=1)

    out_term = product(hidden_all, w_out, False).astype(bf16)
    grad_pairs.append(grad_pair(2))
    grad_rows, out_term = after(grad_rows, out_term)
    output, _ = ring_total(out_term)
    grad_pairs.append(grad_pair(3))
    grad_pre, grad_term = [], 0.0

    def grad_chunk(c):
        return share((added(grad_pairs[c]) * gelu_slope(pre[c])).astype(bf16))

    hidden_all, grad_pairs[3][0] = after(hidden_all, grad_pairs[3][0])
    grad_w_out = inner_rows(hidden_all, grad_rows).astype(bf16)
    grad_pairs[2][1], grad_w_out = after(grad_pairs[2][1], grad_w_out)
    for c in range(CHUNKS):
        grad_pre.append(grad_chunk(c))
        grad_term = grad_term + product(grad_pre[c], columns(c), True)
    grad_w_in = inner_rows(token_rows, jnp.concatenate(grad_pre, axis=1)).astype(bf16)
    grad_tokens, grad_w_in = ring_total(grad_term, grad_w_in)
    return (output, grad_tokens, grad_w_in, grad_w_out)


def solution(mesh):
    in_specs = (P(("groups", "gy"), "gx"), P("gx", "gy"), P("gy", "gx"), P(("groups", "gy"), "gx"))
    out_specs = (
        P(("groups", "gy"), "gx"),
        P(("groups", "gy"), "gx"),
        P(("groups", "gx"), "gy"),
        P(("groups", "gy"), "gx"),
    )
    n_gy = mesh.shape["gy"]
    if mesh.shape["gx"] == 4 and n_gy % 2 == 0:
        shards = lambda *arrays: square_shards(n_gy, *arrays)
    else:
        shards = general_shards
    return jax.shard_map(shards, mesh=mesh, in_specs=in_specs, out_specs=out_specs, check_vma=False)
```
